32 devices in a mesh: ctx: 4 (over y, x), exp: 8 (over z, core).
Axes of the slice: x: 2, y: 2, z: 4, core: 2. Of those that a mesh axis runs over, the one named last changes fastest.
Arguments:
- tokens: bfloat16 [1024, 4096], P('exp', 'ctx'), may hold values from -6 to 6
- cotangent: bfloat16 [1024, 4096], P('exp', 'ctx'), may hold values from -6 to 6
- routes: int32 [1024, 8], P('exp'), may hold values from 0 to 15, all different within a row; in each aligned block of 128 rows (0 to 127, 128 to 255, ...) at most 96 rows name the same one
- router_weight: float32 [4096, 16], P('ctx'), may hold values from -0.09375 to 0.09375
- expert_out: bfloat16 [16, 768, 4096], P('exp', None, 'ctx'), may hold values from -6 to 6
Outputs:
- mixed: bfloat16 [1024, 4096], P('exp', 'ctx')
- token_grad: bfloat16 [1024, 4096], P('exp', 'ctx')
- router_grad: float32 [4096, 16], P('ctx')
- slot_grad: bfloat16 [16, 768, 4096], P('exp', None, 'ctx')
The draws below stay inside these ranges and needn't reach their ends.
Inputs may be any that keep to these rules, and one draw needn't show every extreme that they name: `routes`: each row names 8 different experts; among the rows of one index of exp no expert is named more than 96 times.
All inputs are finite; a program needn't handle non-finite values.
Results may differ from the reference program's by a relative error of at most 0.00105.
Values may be sent and summed in bfloat16 or wider, within the bound.
A program may use at most 64 MiB of HBM per device.

```python
import math
import jax
import jax.numpy as jnp
import numpy as np
from jax import lax

D = 4096
TOP = 8
TOK_DEV = 128
EXPERTS = 16
CAP = 96
TOKENS = 1024
N_EXP = 8


def block_scale(stream_key, shape, split, low, high):
    def one(dim, shards_of):
        draws = jax.random.uniform(jax.random.fold_in(jax.random.fold_in(stream_key, 6), dim), (shards_of,), jnp.float32, low / len(split), high / len(split))
        return jnp.repeat(jnp.exp(draws), shape[dim] // shards_of).reshape((-1,) + (1,) * (len(shape) - dim - 1))

    factor_of = one(*split[0])
    for cut in split[1:]:
        factor_of = factor_of * one(*cut)
    return factor_of


def deal_out(stream_key, own, number, rows, count, top, limit, slope):
    sequence = jax.random.permutation(stream_key, count)
    heavy_load, usual = portions_of(count, rows * top, limit, slope, True), portions_of(count, rows * top, limit, slope, False)
    places = jnp.arange(count)

    def named(tallies, turn):
        used = int((tallies > 0).sum())
        fixed = max(1, used // 4)
        passed = fixed + (places - fixed + turn * (used - fixed)) % max(1, count - fixed)
        return jnp.zeros((count,), jnp.int32).at[sequence[jnp.where(places < fixed, places, passed)]].set(jnp.asarray(tallies, jnp.int32))

    tallies = jnp.where(number % 4 == 0, named(heavy_load, number // 4), named(usual, number - number // 4 - 1))
    mixed = jax.random.permutation(jax.random.fold_in(own, 3), count)
    source_of, receiver = mixed[0:count // 2 * 2:2], mixed[1:count // 2 * 2:2]
    margin = jnp.minimum(tallies[source_of] - 1, limit - tallies[receiver]) // 2
    margin = jnp.where((source_of == sequence[0]) | (receiver == sequence[0]) | (tallies[receiver] == 0), 0, jnp.maximum(margin, 0))
    passed = jax.random.randint(jax.random.fold_in(own, 4), (count // 2,), 0, 1 << 20) % (margin + 1)
    tallies = tallies.at[source_of].add(-passed).at[receiver].add(passed)
    members = jnp.searchsorted(jnp.cumsum(tallies), jnp.arange(rows * top), side="right").astype(jnp.int32)
    listing = members.reshape(top, rows).T
    listing = listing[jax.random.permutation(jax.random.fold_in(own, 1), rows)]
    turn = jax.random.randint(jax.random.fold_in(own, 2), (rows, 1), 0, top)
    return jnp.take_along_axis(listing, (jnp.arange(top)[None, :] + turn) % top, axis=1)


def portions_of(count, total, most, lean, full):
    portions = [(1 << 20) // math.isqrt(rank ** lean) + 1 for rank in range(1, count + 1)]
    largest = most if full else min(most, max(-(-total // count), total * portions[0] // sum(portions)))
    least = 1 if total - largest >= count - 1 else 0
    holding, surplus = [largest] + [least] * (count - 1), total - largest - least * (count - 1)
    while surplus > 0:
        free = [i for i in range(1, count) if holding[i] < largest] or [i for i in range(1, count) if holding[i] < most]
        whole, remaining = sum([portions[i] for i in free]), surplus
        for i in free:
            more = min(most - holding[i], max(1, remaining * portions[i] // whole), surplus)
            holding[i] = holding[i] + more
            surplus = surplus - more
    return np.array(holding)


def scatter_about(rng, extent, scale, most, split=(), kind=jnp.bfloat16):
    drawn = jax.random.normal(rng, extent, jnp.float32) * scale
    if len(split) > 0:
        drawn = block_scale(rng, extent, split, -0.22, 0.18) * drawn
    return jnp.clip(drawn, min=-most, max=most).astype(kind)


def setup_inputs(seed: int = 0) -> dict:
    seeds = jax.random.split(jax.random.key(seed), 6)
    tokens = scatter_about(seeds[0], (TOKENS, D), 1.0, 6.0, ((0, 8), (1, 4)))
    cotangent = scatter_about(seeds[1], (TOKENS, D), 1.0, 6.0, ((0, 8), (1, 4)))
    routes_keys = jax.random.split(jax.random.fold_in(seeds[2], 1), TOKENS // TOK_DEV)
    routes_turns = jax.random.permutation(jax.random.fold_in(seeds[2], 3), TOKENS // TOK_DEV)
    routes = jax.vmap(lambda own, number: deal_out(jax.random.fold_in(seeds[2], 2), own, number, TOK_DEV, EXPERTS, TOP, CAP, 2))(routes_keys, routes_turns).reshape((TOKENS, TOP))
    router_weight = scatter_about(seeds[3], (D, EXPERTS), D ** -0.5, 0.09375, ((0, 4),), jnp.float32)
    expert_out = scatter_about(seeds[4], (EXPERTS, N_EXP * CAP, D), 1.0, 6.0, ((0, 8), (2, 4)))
    return {"tokens": tokens, "cotangent": cotangent, "routes": routes, "router_weight": router_weight, "expert_out": expert_out}


def slot_rows(routes):
    blocks = routes.reshape(N_EXP, TOK_DEV * TOP)
    onehot = (blocks[:, :, None] == jnp.arange(EXPERTS, dtype=jnp.int32)[None, None, :]).astype(jnp.int32)
    earlier = jnp.cumsum(onehot, axis=1) - onehot
    position = jnp.sum(earlier * onehot, axis=2).astype(jnp.int32)
    offsets = (jnp.arange(N_EXP, dtype=jnp.int32) * CAP)[:, None]
    return (offsets + position).reshape(TOKENS, TOP).astype(jnp.int32)


def reference(tokens, cotangent, routes, router_weight, expert_out):
    slot_row = slot_rows(routes)
    highest = lax.Precision.HIGHEST
    logits = jnp.dot(tokens.astype(jnp.float32), router_weight, precision=highest)
    expo = jnp.exp(logits)
    probs = expo / jnp.sum(expo, axis=1, keepdims=True)
    chosen = jnp.take_along_axis(probs, routes, axis=1)
    total = jnp.sum(chosen, axis=1, keepdims=True)
    gates = chosen / total

    def block(inputs):
        cot, chosen_routes, chosen_rows, weights = inputs
        pairs = expert_out[chosen_routes, chosen_rows].astype(jnp.float32)
        mixed_block = jnp.sum(weights[:, :, None] * pairs, axis=1).astype(jnp.bfloat16)
        dot_block = jnp.sum(cot.astype(jnp.float32)[:, None, :] * pairs, axis=2)
        return mixed_block, dot_block

    mixed, dots = lax.map(block, (cotangent.reshape(N_EXP, TOK_DEV, D), routes.reshape(N_EXP, TOK_DEV, TOP),
                                  slot_row.reshape(N_EXP, TOK_DEV, TOP), gates.reshape(N_EXP, TOK_DEV, TOP)))
    mixed = mixed.reshape(TOKENS, D)
    dots = dots.reshape(TOKENS, TOP)
    weighted = (gates[:, :, None] * cotangent.astype(jnp.float32)[:, None, :]).astype(jnp.bfloat16)
    slot_grad = jnp.zeros((EXPERTS, N_EXP * CAP, D), jnp.bfloat16).at[routes, slot_row].set(weighted)
    dchosen = (dots - jnp.sum(dots * gates, axis=1, keepdims=True)) / total
    match = (routes[:, :, None] == jnp.arange(EXPERTS, dtype=jnp.int32)[None, None, :]).astype(jnp.float32)
    spread = jnp.sum(match * dchosen[:, :, None], axis=1)
    dlogits = probs * (spread - jnp.sum(chosen * dchosen, axis=1, keepdims=True))
    token_grad = jnp.dot(dlogits, router_weight.T, precision=highest).astype(jnp.bfloat16)
    router_grad = jnp.dot(tokens.astype(jnp.float32).T, dlogits, precision=highest)
    return mixed, token_grad, router_grad, slot_grad
```

```python
import jax
import jax.numpy as jnp
from jax import lax
from jax.sharding import PartitionSpec as P

HIGHEST = lax.Precision.HIGHEST


def route_slots(routes, experts):
    rows = routes.shape[0]
    match = routes[:, :, None] == jnp.arange(experts, dtype=jnp.int32)[None, None, :]
    mask = jnp.sum(match.astype(jnp.float32), axis=1)
    earlier = jnp.arange(rows)[:, None] > jnp.arange(rows)[None, :]
    slot = jnp.dot(
        earlier.astype(jnp.bfloat16), mask.astype(jnp.bfloat16), preferred_element_type=jnp.float32
    )
    return mask, jnp.where(mask > 0, slot, -1.0)


def body(tokens, cotangent, routes, router_weight, expert_out):
    rows, width = tokens.shape
    local = expert_out.shape[0]
    sources = lax.axis_size("exp")
    experts = local * sources
    capacity = expert_out.shape[1] // sources
    mask, slot = route_slots(routes, experts)
    cot_all = lax.all_gather(cotangent, "exp")
    tokens_wide = tokens.astype(jnp.float32)
    logits = lax.psum(jnp.dot(tokens_wide, router_weight, precision=HIGHEST), "ctx")
    expo = jnp.exp(logits)
    probs = expo / jnp.sum(expo, axis=1, keepdims=True)
    chosen = probs * mask
    total = jnp.sum(chosen, axis=1, keepdims=True)
    gates = chosen / total
    both = jnp.stack([slot.T, gates.T], axis=1).reshape(sources, local, 2, rows)
    both = lax.all_to_all(both, "exp", split_axis=0, concat_axis=0, tiled=True)
    their_slot, their_gate = both[:, :, 0], both[:, :, 1]
    hot = their_slot[:, :, None, :] == jnp.arange(capacity, dtype=jnp.float32)[:, None]
    gathered = jnp.einsum(
        "slct,stw->slcw", hot.astype(jnp.bfloat16), cot_all, preferred_element_type=jnp.float32
    )
    weight = jnp.where(hot, their_gate[:, :, None, :], 0.0)
    slot_gate = jnp.sum(weight, axis=3)
    layout = (local, sources, capacity, width)
    out = jnp.swapaxes(expert_out.reshape(layout), 0, 1).astype(jnp.float32)
    slot_grad = (slot_gate[..., None] * gathered).astype(jnp.bfloat16)
    slot_grad = jnp.swapaxes(slot_grad, 0, 1).reshape(expert_out.shape)
    slot_dots = jnp.sum(gathered * out, axis=3)
    token_dots = jnp.sum(jnp.where(hot, slot_dots[..., None], 0.0), axis=2)
    token_dots = lax.all_to_all(token_dots, "exp", split_axis=0, concat_axis=0, tiled=True)
    dots = lax.psum(token_dots.reshape(experts, rows), "ctx").T
    partial = jnp.einsum("slct,slcw->stw", weight, out, precision=HIGHEST)
    mixed = lax.psum_scatter(partial, "exp", scatter_dimension=0, tiled=False)
    mixed = mixed.astype(jnp.bfloat16)
    dchosen = mask * (dots - jnp.sum(dots * gates, axis=1, keepdims=True)) / total
    dlogits = probs * (dchosen - jnp.sum(chosen * dchosen, axis=1, keepdims=True))
    token_grad = jnp.dot(dlogits, router_weight.T, precision=HIGHEST).astype(jnp.bfloat16)
    router_grad = lax.psum(jnp.dot(tokens_wide.T, dlogits, precision=HIGHEST), "exp")
    return mixed, token_grad, router_grad, slot_grad


def solution(mesh):
    in_specs = (
        P("exp", "ctx"),
        P("exp", "ctx"),
        P("exp", None),
        P("ctx", None),
        P("exp", None, "ctx"),
    )
    out_specs = (P("exp", "ctx"), P("exp", "ctx"), P("ctx", None), P("exp", None, "ctx"))
    return jax.shard_map(body, mesh=mesh, in_specs=in_specs, out_specs=out_specs, check_vma=False)
```

```python
import functools

import jax
import jax.numpy as jnp
from jax import lax
from jax.experimental import pallas as pl
from jax.experimental.pallas import tpu as pltpu
from jax.sharding import PartitionSpec as P

HIGHEST = lax.Precision.HIGHEST
MESH = pl.DeviceIdType.MESH
F32, BF16 = jnp.float32, jnp.bfloat16


def route_slots(routes, experts):
    rows = routes.shape[0]
    match = routes[:, :, None] == jnp.arange(experts, dtype=jnp.int32)[None, None, :]
    mask = jnp.sum(match.astype(jnp.float32), axis=1)
    earlier = jnp.arange(rows)[:, None] > jnp.arange(rows)[None, :]
    slot = jnp.dot(
        earlier.astype(jnp.bfloat16), mask.astype(jnp.bfloat16), preferred_element_type=jnp.float32
    )
    return mask, jnp.where(mask > 0, slot, -1.0)


def body(tokens, cotangent, routes, router_weight, expert_out):
    rows, width = tokens.shape
    local = expert_out.shape[0]
    sources = lax.axis_size("exp")
    experts = local * sources
    capacity = expert_out.shape[1] // sources
    mask, slot = route_slots(routes, experts)
    cot_all = lax.all_gather(cotangent, "exp")
    tokens_wide = tokens.astype(jnp.float32)
    logits = lax.psum(jnp.dot(tokens_wide, router_weight, precision=HIGHEST), "ctx")
    expo = jnp.exp(logits)
    probs = expo / jnp.sum(expo, axis=1, keepdims=True)
    chosen = probs * mask
    total = jnp.sum(chosen, axis=1, keepdims=True)
    gates = chosen / total
    both = jnp.stack([slot.T, gates.T], axis=1).reshape(sources, local, 2, rows)
    both = lax.all_to_all(both, "exp", split_axis=0, concat_axis=0, tiled=True)
    their_slot, their_gate = both[:, :, 0], both[:, :, 1]
    hot = their_slot[:, :, None, :] == jnp.arange(capacity, dtype=jnp.float32)[:, None]
    gathered = jnp.einsum(
        "slct,stw->slcw", hot.astype(jnp.bfloat16), cot_all, preferred_element_type=jnp.float32
    )
    weight = jnp.where(hot, their_gate[:, :, None, :], 0.0)
    slot_gate = jnp.sum(weight, axis=3)
    layout = (local, sources, capacity, width)
    out = jnp.swapaxes(expert_out.reshape(layout), 0, 1).astype(jnp.float32)
    slot_grad = (slot_gate[..., None] * gathered).astype(jnp.bfloat16)
    slot_grad = jnp.swapaxes(slot_grad, 0, 1).reshape(expert_out.shape)
    slot_dots = jnp.sum(gathered * out, axis=3)
    token_dots = jnp.sum(jnp.where(hot, slot_dots[..., None], 0.0), axis=2)
    token_dots = lax.all_to_all(token_dots, "exp", split_axis=0, concat_axis=0, tiled=True)
    dots = lax.psum(token_dots.reshape(experts, rows), "ctx").T
    partial = jnp.einsum("slct,slcw->stw", weight, out, precision=HIGHEST)
    mixed = lax.psum_scatter(partial, "exp", scatter_dimension=0, tiled=False)
    mixed = mixed.astype(jnp.bfloat16)
    dchosen = mask * (dots - jnp.sum(dots * gates, axis=1, keepdims=True)) / total
    dlogits = probs * (dchosen - jnp.sum(chosen * dchosen, axis=1, keepdims=True))
    token_grad = jnp.dot(dlogits, router_weight.T, precision=HIGHEST).astype(jnp.bfloat16)
    router_grad = lax.psum(jnp.dot(tokens_wide.T, dlogits, precision=HIGHEST), "exp")
    return mixed, token_grad, router_grad, slot_grad


def dot(a, b, ca, cb, precision=None):
    return lax.dot_general(
        a, b, (((ca,), (cb,)), ((), ())), precision=precision, preferred_element_type=F32
    )


def kernel(
    n_ctx, sources, tokens, cot, routes, weight, out,
    mixed, token_grad, router_grad, slot_grad,
    cot_all, acc, give, sib, inc, logit, info_out, info, dots_out, dots_in, dots, rg_out, rg_in,
    rg_all, ag_send, ag_recv, sib_send, sib_recv, line_send, line_recv, ctx_send, ctx_recv,
    exp_send, exp_recv,
):
    rows, width = tokens.shape
    local, _, capacity, _ = out.shape
    experts = local * sources
    chips = sources // 2
    last = chips - 1
    me, my_ctx = lax.axis_index("exp"), lax.axis_index("ctx")
    z, core = me // 2, lax.rem(me, 2)
    other = 1 - core
    sibling = 2 * z + other
    exp_peers = [lax.rem(me + d, sources) for d in range(1, sources)]
    ctx_peers = [lax.rem(my_ctx + d, n_ctx) for d in range(1, n_ctx)]

    barrier = pltpu.get_barrier_semaphore()
    for p in exp_peers:
        pl.semaphore_signal(barrier, inc=1, device_id={"exp": p}, device_id_type=MESH)
    for p in ctx_peers:
        pl.semaphore_signal(barrier, inc=1, device_id={"ctx": p}, device_id_type=MESH)
    pl.semaphore_wait(barrier, len(exp_peers) + len(ctx_peers))

    def remote(src, dst, send, recv, **to):
        return pltpu.make_async_remote_copy(
            src_ref=src, dst_ref=dst, send_sem=send, recv_sem=recv,
            device_id=to, device_id_type=MESH,
        )

    def gather(kind, block, to):
        src = cot if kind == "own" else cot_all.at[block]
        return lambda way: remote(
            src, cot_all.at[block], ag_send.at[way, block], ag_recv.at[block], exp=to
        )

    right, left = me + 2, me - 2

    @pl.when(z < last)
    def _():
        gather("own", me, right)(0).start()

    @pl.when(z > 0)
    def _():
        gather("own", me, left)(1).start()

    gather("own", me, sibling)(2).start()

    def to_ctx(step, buf):
        return [
            remote(buf.at[my_ctx], buf.at[my_ctx], ctx_send.at[step, d], ctx_recv.at[step, my_ctx], ctx=p)
            for d, p in enumerate(ctx_peers)
        ], [
            remote(buf.at[p], buf.at[p], ctx_send.at[step, d], ctx_recv.at[step, p], ctx=p)
            for d, p in enumerate(ctx_peers)
        ]

    def to_exp(step, src, dst, gathers=False):
        return [
            remote(src if gathers else src.at[p], dst.at[me], exp_send.at[step, d], exp_recv.at[step, me], exp=p)
            for d, p in enumerate(exp_peers)
        ], [
            remote(dst.at[p], dst.at[p], exp_send.at[step, d], exp_recv.at[step, p], exp=p)
            for d, p in enumerate(exp_peers)
        ]

    def start(pair):
        for c in pair[0]:
            c.start()

    def finish(pair):
        for c in pair[1]:
            c.wait_recv()
        for c in pair[0]:
            c.wait_send()

    wide = tokens[...].astype(F32)
    logit[my_ctx] = dot(weight[...], wide, 1, 1, HIGHEST)
    swap = to_ctx(0, logit)
    start(swap)
    expert = lax.broadcasted_iota(jnp.int32, (experts, rows), 0)
    mask = jnp.zeros((experts, rows), F32)
    for k in range(routes.shape[0]):
        mask += jnp.where(expert == routes[k : k + 1, :], 1.0, 0.0)
    before = lax.broadcasted_iota(jnp.int32, (rows, rows), 0) < lax.broadcasted_iota(
        jnp.int32, (rows, rows), 1
    )
    slot = dot(mask.astype(BF16), jnp.where(before, 1.0, 0.0).astype(BF16), 1, 0)
    slot = jnp.where(mask > 0, slot, -1.0)
    finish(swap)
    expo = jnp.exp(sum(logit[i] for i in range(1, n_ctx)) + logit[0])
    probs = expo / jnp.sum(expo, axis=0, keepdims=True)
    chosen = probs * mask
    total = jnp.sum(chosen, axis=0, keepdims=True)
    gates = chosen / total
    for p in range(sources):
        info_out[p, 0:local] = slot[p * local : (p + 1) * local]
        info_out[p, local : 2 * local] = gates[p * local : (p + 1) * local]
    swap = to_exp(0, info_out, info)
    start(swap)
    info[me] = info_out[me]
    finish(swap)

    capacity_iota = lax.broadcasted_iota(jnp.int32, (capacity, rows), 0).astype(F32)

    def part(source):
        tile = info[source]
        total = None
        for i in range(local):
            gate = tile[local + i : local + i + 1, :]
            rows_of = out[i, source]
            hot = capacity_iota == tile[i : i + 1, :]
            for _ in range(3):
                piece = gate.astype(BF16)
                gate = gate - piece.astype(F32)
                put = jnp.where(hot, piece.astype(F32), 0.0).astype(BF16)
                term = dot(put, rows_of, 0, 0)
                total = term if total is None else total + term
        return total

    def aim(i):
        return jnp.where(2 * z < chips, last - i, i)

    def to_sibling(chip):
        return remote(give.at[chip], sib.at[chip], sib_send.at[chip], sib_recv.at[chip], exp=sibling)

    def along(chip, step):
        to = me + 2 * step
        place = jnp.where((step < 0) & (z - 1 == chip), chips, chip)
        return remote(acc.at[chip], inc.at[place], line_send.at[chip], line_recv.at[place], exp=to)

    def arrived(place):
        remote(inc.at[place], inc.at[place], line_send.at[0], line_recv.at[place], exp=sibling).wait_recv()

    def give_away(i, _):
        chip = aim(i)
        give[chip] = part(2 * chip + other)
        to_sibling(chip).start()
        return _

    lax.fori_loop(0, chips, give_away, 0)

    def keep(i, _):
        chip = aim(i)
        mine = part(2 * chip + core)
        to_sibling(chip).wait_recv()
        acc[chip] = mine + sib[chip]

        @pl.when((z == 0) & (chip > z))
        def _():
            along(chip, 1).start()

        @pl.when((z == last) & (chip < z))
        def _():
            along(chip, -1).start()

        return _

    def keep_loop(i, carry):
        keep(i, 0)
        return carry

    lax.fori_loop(0, chips, keep_loop, 0)

    for d in range(1, chips):

        @pl.when(z >= d)
        def _(d=d):
            block = me - 2 * d
            gather("held", block, sibling)(2).wait_recv()

            @pl.when(z < last)
            def _():
                gather("held", block, right)(0).start()

            gather("held", block, sibling)(2).start()

        @pl.when(z + d <= last)
        def _(d=d):
            block = me + 2 * d
            gather("held", block, sibling)(2).wait_recv()

            @pl.when(z > 0)
            def _():
                gather("held", block, left)(1).start()

            gather("held", block, sibling)(2).start()

    cot_all[me] = cot[...]

    def backward(source, carry):
        @pl.when(lax.rem(source, 2) != core)
        def _():
            gather("held", source, sibling)(2).wait_recv()

        tile = info[source]
        for i in range(local):
            hot = capacity_iota == tile[i : i + 1, :]
            held = dot(jnp.where(hot, 1.0, 0.0).astype(BF16), cot_all[source], 1, 0)
            gate = jnp.sum(jnp.where(hot, tile[local + i : local + i + 1, :], 0.0), axis=1, keepdims=True)
            slot_grad[i, source] = (gate * held).astype(BF16)
            inner = jnp.sum(held * out[i, source].astype(F32), axis=1, keepdims=True)
            dots_out[source, i : i + 1] = jnp.sum(jnp.where(hot, inner, 0.0), axis=0, keepdims=True)
        return carry

    lax.fori_loop(0, sources, backward, 0)
    swap = to_exp(1, dots_out, dots_in)
    start(swap)
    dots_in[me] = dots_out[me]

    def pass_on(turn):
        @pl.when((z > 0) & (last - turn > z))
        def _():
            arrived(last - turn)
            acc[last - turn] += inc[last - turn]
            along(last - turn, 1).start()

        @pl.when((z < last) & (turn < z))
        def _():
            arrived(turn)
            acc[turn] += inc[turn]
            along(turn, -1).start()

    pass_on(0)
    finish(swap)
    for p in range(sources):
        dots[my_ctx, p * local : (p + 1) * local] = dots_in[p, 0:local]
    swap = to_ctx(1, dots)
    start(swap)
    for turn in range(1, last):
        pass_on(turn)
    finish(swap)
    whole = sum(dots[i] for i in range(1, n_ctx)) + dots[0]
    dchosen = mask * ((whole - jnp.sum(whole * gates, axis=0, keepdims=True)) / total)
    dlogits = probs * (dchosen - jnp.sum(chosen * dchosen, axis=0, keepdims=True))
    partial = dot(dlogits, wide, 1, 0, HIGHEST)
    cut = width // sources
    for p in range(sources):
        rg_out[p] = partial[:, p * cut : (p + 1) * cut]
    swap = to_exp(2, rg_out, rg_in)
    start(swap)
    token_grad[...] = dot(dlogits.T, weight[...], 1, 0, HIGHEST).astype(BF16)
    rg_in[me] = rg_out[me]
    finish(swap)
    rg_all[me] = sum(rg_in[i] for i in range(1, sources)) + rg_in[0]
    swap = to_exp(3, rg_all.at[me], rg_all, True)
    start(swap)

    @pl.when(z > 0)
    def _():
        arrived(z)
        acc[z] += inc[z]

    @pl.when(z < last)
    def _():
        arrived(chips)
        acc[z] += inc[chips]

    mixed[...] = acc[z].astype(BF16)
    finish(swap)
    router_grad[...] = rg_all[...]

    def sent(chip, carry):
        to_sibling(chip).wait_send()

        @pl.when(chip != z)
        def _():
            along(chip, 1).wait_send()

        for c in range(2):
            block = 2 * chip + c

            @pl.when(core == c)
            def _():
                gather("held", block, sibling)(2).wait_send()

                @pl.when((chip <= z) & (z < last))
                def _():
                    gather("held", block, right)(0).wait_send()

                @pl.when((chip >= z) & (z > 0))
                def _():
                    gather("held", block, left)(1).wait_send()

        return carry

    lax.fori_loop(0, chips, sent, 0)


def fused(n_ctx, sources, tokens, cotangent, routes, router_weight, expert_out):
    rows, width = tokens.shape
    local = expert_out.shape[0]
    capacity = expert_out.shape[1] // sources
    experts, chips, cut = local * sources, sources // 2, width // sources
    tile = -(-2 * local // 8) * 8
    vmem = pl.BlockSpec(memory_space=pltpu.VMEM)
    dma = pltpu.SemaphoreType.DMA
    mixed, token_grad, router_grad, slot_grad = pl.pallas_call(
        functools.partial(kernel, n_ctx, sources),
        out_shape=(
            jax.ShapeDtypeStruct((rows, width), BF16),
            jax.ShapeDtypeStruct((rows, width), BF16),
            jax.ShapeDtypeStruct((sources, experts, cut), F32),
            jax.ShapeDtypeStruct((local, sources, capacity, width), BF16),
        ),
        in_specs=[vmem] * 5,
        out_specs=(vmem,) * 4,
        scratch_shapes=[
            pltpu.VMEM((sources, rows, width), BF16),
            pltpu.VMEM((chips, rows, width), F32),
            pltpu.VMEM((chips, rows, width), F32),
            pltpu.VMEM((chips, rows, width), F32),
            pltpu.VMEM((chips + 1, rows, width), F32),
            pltpu.VMEM((n_ctx, experts, rows), F32),
            pltpu.VMEM((sources, tile, rows), F32),
            pltpu.VMEM((sources, tile, rows), F32),
            pltpu.VMEM((sources, tile, rows), F32),
            pltpu.VMEM((sources, tile, rows), F32),
            pltpu.VMEM((n_ctx, experts, rows), F32),
            pltpu.VMEM((sources, experts, cut), F32),
            pltpu.VMEM((sources, experts, cut), F32),
            pltpu.VMEM((sources, experts, cut), F32),
            dma((3, sources)),
            dma((sources,)),
            dma((chips,)),
            dma((chips,)),
            dma((chips,)),
            dma((chips + 1,)),
            dma((2, n_ctx)),
            dma((2, n_ctx)),
            dma((4, sources)),
            dma((4, sources)),
        ],
        compiler_params=pltpu.CompilerParams(
            collective_id=0, has_side_effects=True, vmem_limit_bytes=48 * 2**20
        ),
    )(
        tokens,
        cotangent,
        routes.T,
        router_weight.T,
        expert_out.reshape(local, sources, capacity, width),
    )
    router_grad = jnp.swapaxes(router_grad, 1, 2).reshape(router_weight.shape)
    return mixed, token_grad, router_grad, slot_grad.reshape(expert_out.shape)


def solution(mesh):
    n_ctx, sources = mesh.shape["ctx"], mesh.shape["exp"]

    def step(*args):
        tokens, _, _, _, expert_out = args
        rows, width = tokens.shape
        capacity = expert_out.shape[1] // sources
        small = sources <= 8 and sources % 2 == 0 and n_ctx > 1
        if small and capacity % 16 == 0 and rows % 128 == 0 and width % (128 * sources) == 0:
            return fused(n_ctx, sources, *args)
        return body(*args)

    in_specs = (
        P("exp", "ctx"),
        P("exp", "ctx"),
        P("exp", None),
        P("ctx", None),
        P("exp", None, "ctx"),
    )
    out_specs = (P("exp", "ctx"), P("exp", "ctx"), P("ctx", None), P("exp", None, "ctx"))
    return jax.shard_map(step, mesh=mesh, in_specs=in_specs, out_specs=out_specs, check_vma=False)
```

```python
import functools

import jax
import jax.numpy as jnp
from jax import lax
from jax.experimental import pallas as pl
from jax.experimental.pallas import tpu as pltpu
from jax.sharding import PartitionSpec as P

HIGHEST = lax.Precision.HIGHEST
MESH = pl.DeviceIdType.MESH
F32, BF16 = jnp.float32, jnp.bfloat16


def route_slots(routes, experts):
    rows = routes.shape[0]
    match = routes[:, :, None] == jnp.arange(experts, dtype=jnp.int32)[None, None, :]
    mask = jnp.sum(match.astype(jnp.float32), axis=1)
    earlier = jnp.arange(rows)[:, None] > jnp.arange(rows)[None, :]
    slot = jnp.dot(
        earlier.astype(jnp.bfloat16), mask.astype(jnp.bfloat16), preferred_element_type=jnp.float32
    )
    return mask, jnp.where(mask > 0, slot, -1.0)


def body(tokens, cotangent, routes, router_weight, expert_out):
    rows, width = tokens.shape
    local = expert_out.shape[0]
    sources = lax.axis_size("exp")
    experts = local * sources
    capacity = expert_out.shape[1] // sources
    mask, slot = route_slots(routes, experts)
    cot_all = lax.all_gather(cotangent, "exp")
    tokens_wide = tokens.astype(jnp.float32)
    logits = lax.psum(jnp.dot(tokens_wide, router_weight, precision=HIGHEST), "ctx")
    expo = jnp.exp(logits)
    probs = expo / jnp.sum(expo, axis=1, keepdims=True)
    chosen = probs * mask
    total = jnp.sum(chosen, axis=1, keepdims=True)
    gates = chosen / total
    both = jnp.stack([slot.T, gates.T], axis=1).reshape(sources, local, 2, rows)
    both = lax.all_to_all(both, "exp", split_axis=0, concat_axis=0, tiled=True)
    their_slot, their_gate = both[:, :, 0], both[:, :, 1]
    hot = their_slot[:, :, None, :] == jnp.arange(capacity, dtype=jnp.float32)[:, None]
    gathered = jnp.einsum(
        "slct,stw->slcw", hot.astype(jnp.bfloat16), cot_all, preferred_element_type=jnp.float32
    )
    weight = jnp.where(hot, their_gate[:, :, None, :], 0.0)
    slot_gate = jnp.sum(weight, axis=3)
    layout = (local, sources, capacity, width)
    out = jnp.swapaxes(expert_out.reshape(layout), 0, 1).astype(jnp.float32)
    slot_grad = (slot_gate[..., None] * gathered).astype(jnp.bfloat16)
    slot_grad = jnp.swapaxes(slot_grad, 0, 1).reshape(expert_out.shape)
    slot_dots = jnp.sum(gathered * out, axis=3)
    token_dots = jnp.sum(jnp.where(hot, slot_dots[..., None], 0.0), axis=2)
    token_dots = lax.all_to_all(token_dots, "exp", split_axis=0, concat_axis=0, tiled=True)
    dots = lax.psum(token_dots.reshape(experts, rows), "ctx").T
    partial = jnp.einsum("slct,slcw->stw", weight, out, precision=HIGHEST)
    mixed = lax.psum_scatter(partial, "exp", scatter_dimension=0, tiled=False)
    mixed = mixed.astype(jnp.bfloat16)
    dchosen = mask * (dots - jnp.sum(dots * gates, axis=1, keepdims=True)) / total
    dlogits = probs * (dchosen - jnp.sum(chosen * dchosen, axis=1, keepdims=True))
    token_grad = jnp.dot(dlogits, router_weight.T, precision=HIGHEST).astype(jnp.bfloat16)
    router_grad = lax.psum(jnp.dot(tokens_wide.T, dlogits, precision=HIGHEST), "exp")
    return mixed, token_grad, router_grad, slot_grad


def dot(a, b, ca, cb, precision=None):
    return lax.dot_general(
        a, b, (((ca,), (cb,)), ((), ())), precision=precision, preferred_element_type=F32
    )


def kernel(
    n_ctx, sources, tokens_hbm, cot, routes_hbm, weight_hbm, out_hbm,
    mixed, token_grad, router_grad, slot_grad,
    cot_all, acc, give, sib, inc, logit, info_out, info, dots_out, dots_in, dots, rg_out, rg_in,
    rg_all, tokens, routes, weight, out, in_sem, ag_send, ag_recv, sib_send, sib_recv, line_send, line_recv, ctx_send, ctx_recv,
    exp_send, exp_recv,
):
    rows, width = tokens.shape
    local, _, capacity, _ = out.shape
    experts = local * sources
    chips, halves, half = acc.shape[0], acc.shape[1], acc.shape[3]
    last = chips - 1
    me, my_ctx = lax.axis_index("exp"), lax.axis_index("ctx")
    z, core = me // 2, lax.rem(me, 2)
    other = 1 - core
    sibling = 2 * z + other
    exp_peers = [lax.rem(me + d, sources) for d in range(1, sources)]
    ctx_peers = [lax.rem(my_ctx + d, n_ctx) for d in range(1, n_ctx)]

    loads = [
        pltpu.make_async_copy(a, b, in_sem.at[i])
        for i, (a, b) in enumerate(
            [
                (tokens_hbm, tokens),
                (weight_hbm, weight),
                (routes_hbm, routes),
                (out_hbm, out),
                (cot, cot_all.at[me]),
            ]
        )
    ]
    for load in loads:
        load.start()

    barrier = pltpu.get_barrier_semaphore()
    for p in exp_peers:
        pl.semaphore_signal(barrier, inc=1, device_id={"exp": p}, device_id_type=MESH)
    for p in ctx_peers:
        pl.semaphore_signal(barrier, inc=1, device_id={"ctx": p}, device_id_type=MESH)
    pl.semaphore_wait(barrier, len(exp_peers) + len(ctx_peers))

    def remote(src, dst, send, recv, **to):
        return pltpu.make_async_remote_copy(
            src_ref=src, dst_ref=dst, send_sem=send, recv_sem=recv,
            device_id=to, device_id_type=MESH,
        )

    def gather(kind, block, to):
        src = cot if kind == "own" else cot_all.at[block]
        return lambda way: remote(
            src, cot_all.at[block], ag_send.at[way, block], ag_recv.at[block], exp=to
        )

    right, left = me + 2, me - 2

    @pl.when(z < last)
    def _():
        gather("own", me, right)(0).start()

    @pl.when(z > 0)
    def _():
        gather("own", me, left)(1).start()

    gather("own", me, sibling)(2).start()

    def to_ctx(step, buf):
        return [
            remote(buf.at[my_ctx], buf.at[my_ctx], ctx_send.at[step, d], ctx_recv.at[step, my_ctx], ctx=p)
            for d, p in enumerate(ctx_peers)
        ], [
            remote(buf.at[p], buf.at[p], ctx_send.at[step, d], ctx_recv.at[step, p], ctx=p)
            for d, p in enumerate(ctx_peers)
        ]

    def to_exp(step, src, dst, gathers=False):
        return [
            remote(src if gathers else src.at[p], dst.at[me], exp_send.at[step, d], exp_recv.at[step, me], exp=p)
            for d, p in enumerate(exp_peers)
        ], [
            remote(dst.at[p], dst.at[p], exp_send.at[step, d], exp_recv.at[step, p], exp=p)
            for d, p in enumerate(exp_peers)
        ]

    def start(pair):
        for c in pair[0]:
            c.start()

    def finish(pair):
        for c in pair[1]:
            c.wait_recv()
        for c in pair[0]:
            c.wait_send()

    for load in loads[:3]:
        load.wait()
    wide = tokens[...].astype(F32)
    logit[my_ctx] = dot(weight[...], wide, 1, 1, HIGHEST)
    swap = to_ctx(0, logit)
    start(swap)
    expert = lax.broadcasted_iota(jnp.int32, (experts, rows), 0)
    mask = jnp.zeros((experts, rows), F32)
    for k in range(routes.shape[0]):
        mask += jnp.where(expert == routes[k : k + 1, :], 1.0, 0.0)
    before = lax.broadcasted_iota(jnp.int32, (rows, rows), 0) < lax.broadcasted_iota(
        jnp.int32, (rows, rows), 1
    )
    slot = dot(mask.astype(BF16), jnp.where(before, 1.0, 0.0).astype(BF16), 1, 0)
    slot = jnp.where(mask > 0, slot, -1.0)
    finish(swap)
    expo = jnp.exp(sum(logit[i] for i in range(1, n_ctx)) + logit[0])
    probs = expo / jnp.sum(expo, axis=0, keepdims=True)
    chosen = probs * mask
    total = jnp.sum(chosen, axis=0, keepdims=True)
    gates = chosen / total
    for p in range(sources):
        info_out[p, 0:local] = slot[p * local : (p + 1) * local]
        info_out[p, local : 2 * local] = gates[p * local : (p + 1) * local]
    swap = to_exp(0, info_out, info)
    start(swap)
    info[me] = info_out[me]
    loads[3].wait()
    loads[4].wait()
    finish(swap)

    capacity_iota = lax.broadcasted_iota(jnp.int32, (capacity, rows), 0).astype(F32)

    pair_iota = lax.broadcasted_iota(jnp.int32, (rows, local * capacity), 1).astype(F32)

    def part(source):
        tile = info[source].T
        gate = jnp.zeros(pair_iota.shape, F32)
        for i in range(local):
            slot_i = tile[:, i : i + 1]
            place = jnp.where(slot_i >= 0, slot_i + float(i * capacity), -1.0)
            gate = jnp.where(pair_iota == place, tile[:, local + i : local + i + 1], gate)
        rows_of = jnp.concatenate([out[i, source] for i in range(local)], axis=0)
        total = None
        for _ in range(3):
            piece = gate.astype(BF16)
            gate = gate - piece.astype(F32)
            term = dot(piece, rows_of, 1, 0)
            total = term if total is None else total + term
        return total

    def aim(i):
        return jnp.where(2 * z < chips, last - i, i)

    def to_sibling(chip):
        return remote(give.at[chip], sib.at[chip], sib_send.at[chip], sib_recv.at[chip], exp=sibling)

    def along(chip, h, step):
        to = me + 2 * step
        place = jnp.where((step < 0) & (z - 1 == chip), chips, chip)
        return remote(
            acc.at[chip, h], inc.at[place, h], line_send.at[chip, h], line_recv.at[place, h], exp=to
        )

    def arrived(place, h):
        remote(
            inc.at[place, h], inc.at[place, h], line_send.at[0, h], line_recv.at[place, h], exp=sibling
        ).wait_recv()

    def first_hop(turn, h):
        @pl.when(z == 0)
        def _():
            along(last - turn, h, 1).start()

        @pl.when(z == last)
        def _():
            along(turn, h, -1).start()

    def give_away(i):
        chip = aim(i)
        give[chip] = part(2 * chip + other)
        to_sibling(chip).start()

    def keep(i):
        chip = aim(i)
        mine = part(2 * chip + core)
        to_sibling(chip).wait_recv()
        for h in range(halves):
            cols = slice(h * half, (h + 1) * half)
            acc[chip, h] = mine[:, cols] + sib[chip, :, cols]

    give_away(0)
    keep(0)
    for h in range(halves):
        first_hop(0, h)

    def give_and_keep(i, carry):
        give_away(i)
        keep(i)
        return carry

    lax.fori_loop(1, chips, give_and_keep, 0)

    for d in range(1, chips):

        @pl.when(z >= d)
        def _(d=d):
            block = me - 2 * d
            gather("held", block, sibling)(2).wait_recv()

            @pl.when(z < last)
            def _():
                gather("held", block, right)(0).start()

            gather("held", block, sibling)(2).start()

        @pl.when(z + d <= last)
        def _(d=d):
            block = me + 2 * d
            gather("held", block, sibling)(2).wait_recv()

            @pl.when(z > 0)
            def _():
                gather("held", block, left)(1).start()

            gather("held", block, sibling)(2).start()

    def pass_on(turn, h):
        @pl.when((z > 0) & (last - turn > z))
        def _():
            arrived(last - turn, h)
            acc[last - turn, h] += inc[last - turn, h]
            along(last - turn, h, 1).start()

        @pl.when((z < last) & (turn < z))
        def _():
            arrived(turn, h)
            acc[turn, h] += inc[turn, h]
            along(turn, h, -1).start()

    def backward(source, carry):
        turn, h = source // halves, lax.rem(source, halves)

        @pl.when(turn + 1 < last)
        def _():
            for step, end, chip in ((1, 0, last - turn), (-1, last, turn)):

                @pl.when(z == end)
                def _(step=step, chip=chip):
                    along(chip, h, step).wait_send()

            first_hop(turn + 1, h)

        @pl.when(turn < last)
        def _():
            pass_on(turn, h)

        @pl.when(lax.rem(source, 2) != core)
        def _():
            gather("held", source, sibling)(2).wait_recv()

        tile = info[source]
        for i in range(local):
            hot = capacity_iota == tile[i : i + 1, :]
            held = dot(jnp.where(hot, 1.0, 0.0).astype(BF16), cot_all[source], 1, 0)
            gate = jnp.sum(jnp.where(hot, tile[local + i : local + i + 1, :], 0.0), axis=1, keepdims=True)
            slot_grad[i, source] = (gate * held).astype(BF16)
            inner = jnp.sum(held * out[i, source].astype(F32), axis=1, keepdims=True)
            dots_out[source, i : i + 1] = jnp.sum(jnp.where(hot, inner, 0.0), axis=0, keepdims=True)
        return carry

    lax.fori_loop(0, sources, backward, 0)
    swap = to_exp(1, dots_out, dots_in)
    start(swap)
    dots_in[me] = dots_out[me]
    finish(swap)
    for p in range(sources):
        dots[my_ctx, p * local : (p + 1) * local] = dots_in[p, 0:local]
    swap = to_ctx(1, dots)
    start(swap)
    finish(swap)
    whole = sum(dots[i] for i in range(1, n_ctx)) + dots[0]
    dchosen = mask * ((whole - jnp.sum(whole * gates, axis=0, keepdims=True)) / total)
    dlogits = probs * (dchosen - jnp.sum(chosen * dchosen, axis=0, keepdims=True))
    partial = dot(dlogits, wide, 1, 0, HIGHEST)
    cut = width // sources
    for p in range(sources):
        rg_out[p] = partial[:, p * cut : (p + 1) * cut]
    swap = to_exp(2, rg_out, rg_in)
    start(swap)
    token_grad[...] = dot(dlogits.T, weight[...], 1, 0, HIGHEST).astype(BF16)
    rg_in[me] = rg_out[me]
    finish(swap)
    rg_all[me] = sum(rg_in[i] for i in range(1, sources)) + rg_in[0]
    swap = to_exp(3, rg_all.at[me], rg_all, True)
    start(swap)

    for h in range(halves):

        @pl.when(z > 0)
        def _(h=h):
            arrived(z, h)
            acc[z, h] += inc[z, h]

        @pl.when(z < last)
        def _(h=h):
            arrived(chips, h)
            acc[z, h] += inc[chips, h]

        mixed[:, h * half : (h + 1) * half] = acc[z, h].astype(BF16)
    finish(swap)
    router_grad[...] = rg_all[...]

    def sent(chip, carry):
        to_sibling(chip).wait_send()

        hop = jnp.where(z == 0, 1, last - 1)
        near = ((z > 0) & (z < last)) | (chip == hop)

        @pl.when((chip != z) & near)
        def _():
            for h in range(halves):
                along(chip, h, 1).wait_send()

        for c in range(2):
            block = 2 * chip + c

            @pl.when(core == c)
            def _():
                gather("held", block, sibling)(2).wait_send()

                @pl.when((chip <= z) & (z < last))
                def _():
                    gather("held", block, right)(0).wait_send()

                @pl.when((chip >= z) & (z > 0))
                def _():
                    gather("held", block, left)(1).wait_send()

        return carry

    lax.fori_loop(0, chips, sent, 0)


def fused(n_ctx, sources, tokens, cotangent, routes, router_weight, expert_out):
    rows, width = tokens.shape
    local = expert_out.shape[0]
    capacity = expert_out.shape[1] // sources
    experts, chips, cut = local * sources, sources // 2, width // sources
    tile = -(-2 * local // 8) * 8
    halves = 2
    vmem = pl.BlockSpec(memory_space=pltpu.VMEM)
    dma = pltpu.SemaphoreType.DMA
    mixed, token_grad, router_grad, slot_grad = pl.pallas_call(
        functools.partial(kernel, n_ctx, sources),
        out_shape=(
            jax.ShapeDtypeStruct((rows, width), BF16),
            jax.ShapeDtypeStruct((rows, width), BF16),
            jax.ShapeDtypeStruct((sources, experts, cut), F32),
            jax.ShapeDtypeStruct((local, sources, capacity, width), BF16),
        ),
        in_specs=[pl.BlockSpec(memory_space=pltpu.HBM)] * 5,
        out_specs=(vmem,) * 4,
        scratch_shapes=[
            pltpu.VMEM((sources, rows, width), BF16),
            pltpu.VMEM((chips, halves, rows, width // halves), F32),
            pltpu.VMEM((chips, rows, width), F32),
            pltpu.VMEM((chips, rows, width), F32),
            pltpu.VMEM((chips + 1, halves, rows, width // halves), F32),
            pltpu.VMEM((n_ctx, experts, rows), F32),
            pltpu.VMEM((sources, tile, rows), F32),
            pltpu.VMEM((sources, tile, rows), F32),
            pltpu.VMEM((sources, tile, rows), F32),
            pltpu.VMEM((sources, tile, rows), F32),
            pltpu.VMEM((n_ctx, experts, rows), F32),
            pltpu.VMEM((sources, experts, cut), F32),
            pltpu.VMEM((sources, experts, cut), F32),
            pltpu.VMEM((sources, experts, cut), F32),
            pltpu.VMEM((rows, width), BF16),
            pltpu.VMEM(routes.shape[::-1], jnp.int32),
            pltpu.VMEM(router_weight.shape[::-1], F32),
            pltpu.VMEM((local, sources, capacity, width), BF16),
            dma((5,)),
            dma((3, sources)),
            dma((sources,)),
            dma((chips,)),
            dma((chips,)),
            dma((chips, halves)),
            dma((chips + 1, halves)),
            dma((2, n_ctx)),
            dma((2, n_ctx)),
            dma((4, sources)),
            dma((4, sources)),
        ],
        compiler_params=pltpu.CompilerParams(
            collective_id=0, has_side_effects=True, vmem_limit_bytes=48 * 2**20
        ),
    )(
        tokens,
        cotangent,
        routes.T,
        router_weight.T,
        expert_out.reshape(local, sources, capacity, width),
    )
    router_grad = jnp.swapaxes(router_grad, 1, 2).reshape(router_weight.shape)
    return mixed, token_grad, router_grad, slot_grad.reshape(expert_out.shape)


def solution(mesh):
    n_ctx, sources = mesh.shape["ctx"], mesh.shape["exp"]

    def step(*args):
        tokens, _, _, _, expert_out = args
        rows, width = tokens.shape
        capacity = expert_out.shape[1] // sources
        small = sources in (4, 6, 8) and n_ctx > 1
        if small and capacity % 16 == 0 and rows % 128 == 0 and width % (128 * sources) == 0:
            return fused(n_ctx, sources, *args)
        return body(*args)

    in_specs = (
        P("exp", "ctx"),
        P("exp", "ctx"),
        P("exp", None),
        P("ctx", None),
        P("exp", None, "ctx"),
    )
    out_specs = (P("exp", "ctx"), P("exp", "ctx"), P("ctx", None), P("exp", None, "ctx"))
    return jax.shard_map(step, mesh=mesh, in_specs=in_specs, out_specs=out_specs, check_vma=False)
```
